32 devices in a mesh: oct: 32 (over z, y, x, core).
Axes of the slice: x: 2, y: 2, z: 4, core: 2. Of those that a mesh axis runs over, the one named last changes fastest.
Arguments:
- leaf_spectra: bfloat16 [8192, 2016], P('oct'), may hold values from -6 to 6
- leaf_keys: int32 [8192], P('oct'), may hold values from 8 to 49159, as said below
- parent_keys: int32 [2048], P('oct'), may hold values from 1 to 6144, as said below
- child_phase: float32 [8, 1008], replicated, may hold values from -3.140625 to 3.140625
- coarsen: bfloat16 [2, 1008, 1008], replicated, may hold values from -0.0625 to 0.0625
- transfer: bfloat16 [316, 2016], replicated, may hold values from -0.3125 to 0.3125
- vlist_src: int32 [2048, 189], P('oct'), may hold values from -1 to 511, as said below
- vlist_type: int32 [2048, 189], P('oct'), may hold values from 0 to 315
Outputs:
- upward: bfloat16 [2048, 2016], P('oct')
- local_field: bfloat16 [2048, 2016], P('oct')
The draws below stay inside these ranges and needn't reach their ends.
Inputs may be any that keep to these rules, and one draw needn't show every extreme that they name: leaf_keys: strictly increasing. Every leaf_keys // 8 is a value of parent_keys. The leaves of a parent lie on the device that owns it, except that some of the leaves of a device's last parent (at least one, at most two) are the first leaves of the next device; every device but the first begins so, and the last device's parents have all their leaves at home. parent_keys: strictly increasing; every parent has 1 to 8 leaves. `vlist_src`: in each row the live entries come first, then -1. A live entry is the index of a source parent within the target's window: the 512 parents that end with the last parent of the target's block of 64, counted cyclically. Every target has at least 94 live entries, and on every device some target has all 189 live.
All inputs are finite; a program needn't handle non-finite values.
Results may differ from the reference program's by a relative error of at most 0.0058.
Values may be sent and summed in bfloat16 or wider, within the bound.
A program may use at most 64 MiB of HBM per device.

```python
import math
import jax
import jax.numpy as jnp
from jax import lax

Q = 1008
PAR_DEV = 64
K = 189
OFFS = 316
GROUP = 512
PARENTS = 2048
LEAVES = 8192
N_OCT = 32


def tree_keys(key):
    base_key = jax.random.fold_in(key, 7001)
    key_gap, key_head, key_inner, key_code = jax.random.split(base_key, 4)
    gaps = jax.random.randint(key_gap, (PARENTS,), 1, 4)
    parent_list = jnp.cumsum(gaps).astype(jnp.int32)
    parent_list = (parent_list + 3 * PARENTS - parent_list[PARENTS - 1]).astype(jnp.int32)
    heads = jax.random.randint(key_head, (N_OCT + 1,), 1, 3)
    heads = heads.at[0].set(0).at[N_OCT].set(0)
    inner = jax.random.randint(key_inner, (N_OCT, PAR_DEV + 1), 0, 3)
    inner = inner.at[:, 0].set(0)
    inner = inner.at[:, PAR_DEV].set(heads[:-1] - heads[1:])
    counts = (4 + inner[:, :-1] - inner[:, 1:]).reshape(PARENTS)
    scores = jax.random.randint(key_code, (PARENTS, 8), 0, 1 << 20) * 8 + jnp.arange(8, dtype=jnp.int32)[None, :]
    scores = scores.at[PARENTS - 1, 7].set(-1)
    ranks = jnp.argsort(jnp.argsort(scores, axis=1, stable=True), axis=1, stable=True)
    chosen = ranks < counts[:, None]
    flat_keys = (parent_list[:, None] * 8 + jnp.arange(8, dtype=jnp.int32)[None, :]).reshape(-1)
    positions = jnp.nonzero(chosen.reshape(-1), size=LEAVES)[0]
    return (flat_keys[positions].astype(jnp.int32), parent_list)


def draw_leaf_keys(key, part):
    return tree_keys(key)[0]


def draw_parent_keys(key, part):
    return tree_keys(key)[1]


def draw_vlist_src(key, part):
    key_length, key_value = jax.random.split(jax.random.fold_in(key, 7013))
    lengths = jax.random.randint(key_length, (PARENTS,), K // 2, K + 1)
    lengths = jnp.where(jnp.arange(PARENTS) % PAR_DEV == 0, K, lengths)
    values = jax.random.randint(key_value, (PARENTS, K), 0, GROUP)
    return jnp.where(jnp.arange(K)[None, :] < lengths[:, None], values, -1).astype(jnp.int32)


def with_ends(drawn, own_key, low, top_value):
    dims = drawn.shape
    index_at = [jax.random.randint(jax.random.fold_in(own_key, axis), (), 0, dims[axis]) for axis in range(len(dims))]
    drawn = drawn.at[tuple(index_at)].set(low)
    longest = dims.index(max(dims))
    index_at[longest] = (index_at[longest] + 1) % dims[longest]
    return drawn.at[tuple(index_at)].set(top_value)


def level_of(rng, extent, cuts, smallest, top_value):
    def one(position, parts):
        heights = jax.random.uniform(jax.random.fold_in(jax.random.fold_in(rng, 6), position), (parts,), jnp.float32, smallest / len(cuts), top_value / len(cuts))
        return jnp.repeat(jnp.exp(heights), extent[position] // parts).reshape((-1,) + (1,) * (len(extent) - position - 1))

    level = one(*cuts[0])
    for cut in cuts[1:]:
        level = level * one(*cut)
    return level


def noise(own_key, dims, width, limit, cuts=(), held_as=jnp.bfloat16):
    entries = jax.random.normal(own_key, dims, jnp.float32) * width
    if len(cuts) > 0:
        entries = level_of(own_key, dims, cuts, -0.22, 0.18) * entries
    return jnp.clip(entries, min=-limit, max=limit).astype(held_as)


def setup_inputs(seed: int = 0) -> dict:
    key_of = jax.random.split(jax.random.key(seed), 9)
    leaf_spectra = noise(key_of[0], (LEAVES, 2 * Q), 1.0, 6.0, ((0, 32),))
    leaf_keys = draw_leaf_keys(jax.random.fold_in(key_of[8], 71), 0)
    parent_keys = draw_parent_keys(jax.random.fold_in(key_of[8], 71), 0)
    child_phase = jnp.clip(jax.random.uniform(key_of[3], (8, Q), jnp.float32, -3.140625, 3.140625), -3.140625, 3.140625)
    coarsen = noise(key_of[4], (2, Q, Q), (8 * Q) ** -0.5, 0.0625)
    transfer = noise(key_of[5], (OFFS, 2 * Q), (2 * K) ** -0.5, 0.3125)
    vlist_src = draw_vlist_src(jax.random.fold_in(key_of[8], 71), 0)
    vlist_type = with_ends(jax.random.randint(key_of[7], (PARENTS, K), 0, OFFS), jax.random.fold_in(key_of[7], 1), 0, OFFS - 1).astype(jnp.int32)
    return {"leaf_spectra": leaf_spectra, "leaf_keys": leaf_keys, "parent_keys": parent_keys, "child_phase": child_phase, "coarsen": coarsen, "transfer": transfer, "vlist_src": vlist_src, "vlist_type": vlist_type}


def twist(leaf_spectra, child_phase, child_code):
    angles = child_phase[child_code]
    cosine = jnp.cos(angles)
    sine_part = jnp.sin(angles)
    spectra = leaf_spectra.astype(jnp.float32)
    real_in = spectra[:, :Q]
    imag_in = spectra[:, Q:]
    return jnp.concatenate([real_in * cosine - imag_in * sine_part, real_in * sine_part + imag_in * cosine], 1)


def coarsen_apply(gathered_b, coarsen):
    real_in = gathered_b[:, :Q]
    imag_in = gathered_b[:, Q:]
    real_out = jnp.dot(real_in, coarsen[0], preferred_element_type=jnp.float32) - jnp.dot(imag_in, coarsen[1], preferred_element_type=jnp.float32)
    imag_out = jnp.dot(real_in, coarsen[1], preferred_element_type=jnp.float32) + jnp.dot(imag_in, coarsen[0], preferred_element_type=jnp.float32)
    return jnp.concatenate([real_out, imag_out], 1).astype(jnp.bfloat16)


def reference(leaf_spectra, leaf_keys, parent_keys, child_phase, coarsen, transfer, vlist_src, vlist_type):
    child_code = leaf_keys % 8
    parent_of = leaf_keys // 8
    twisted = twist(leaf_spectra, child_phase, child_code)
    owner_index = jnp.searchsorted(parent_keys, parent_of).astype(jnp.int32)
    gathered = jax.ops.segment_sum(twisted, owner_index, num_segments=PARENTS)
    gathered_b = gathered.astype(jnp.bfloat16)
    upward = coarsen_apply(gathered_b, coarsen)
    block_rows = math.gcd(PARENTS, 64)
    block_count = PARENTS // block_rows

    def one_block(block_index):
        start = block_index * block_rows
        sources = lax.dynamic_slice_in_dim(vlist_src, start, block_rows, 0)
        kinds = lax.dynamic_slice_in_dim(vlist_type, start, block_rows, 0)
        targets = start + jnp.arange(block_rows, dtype=jnp.int32)
        window_base = (targets // PAR_DEV) * PAR_DEV - GROUP + PAR_DEV
        global_src = (window_base[:, None] + jnp.maximum(sources, 0) + PARENTS) % PARENTS
        live_mask = sources >= 0
        source_rows = upward[global_src.astype(jnp.int32)].astype(jnp.float32)
        coefficient = transfer[kinds].astype(jnp.float32)
        real_part = coefficient[..., :Q] * source_rows[..., :Q] - coefficient[..., Q:] * source_rows[..., Q:]
        imag_part = coefficient[..., :Q] * source_rows[..., Q:] + coefficient[..., Q:] * source_rows[..., :Q]
        products = jnp.concatenate([real_part, imag_part], -1)
        return jnp.sum(jnp.where(live_mask[..., None], products, jnp.float32(0.0)), 1)

    results = lax.map(one_block, jnp.arange(block_count, dtype=jnp.int32))
    local_field = results.reshape(PARENTS, 2 * Q).astype(jnp.bfloat16)
    return upward, local_field
```

```python
import functools
import jax
import jax.numpy as jnp
from jax import lax
from jax.experimental import pallas as pl
from jax.experimental.pallas import tpu as pltpu
from jax.sharding import PartitionSpec as P

GBITS = 3
LANES = 128
CHUNK = 32
GROUP = 4


def passed_along(value, axis, steps):
    count = lax.axis_size(axis)
    first, last = (max(0, -steps), min(count, count - steps))
    return lax.ppermute(value, axis, [(source, source + steps) for source in range(first, last)])


def from_behind(block, axis, distance):
    devices = range(lax.axis_size(axis))
    route = [((i - distance) % len(devices), i) for i in devices]
    return lax.ppermute(block, axis, route)


def tiled(values, half_width, width):
    rows = values.shape[0]
    halves = values.reshape(rows, 2, half_width)
    halves = jnp.pad(halves, ((0, 0), (0, 0), (0, width - half_width)))
    return halves.reshape(rows, 2 * width // LANES, LANES)


def interact_kernel(fixed, chunk, half_width, count_ref, src_ref, kind_ref, table_ref, coef_ref, out_ref, sums):
    rows = table_ref.shape[1]
    half = rows // 2

    def some_slots(target, first, count, acc):
        re, im = acc
        for start in range(0, count, GROUP):
            ones, twos = [], []
            for slot in range(start, start + GROUP):
                source = table_ref[src_ref[target, first + slot]]
                kind = kind_ref[target, first + slot]
                ones.append(coef_ref[kind, :rows] * source)
                twos.append(coef_ref[kind, rows:] * source)
            while len(ones) > 1:
                ones = [ones[i] + ones[i + 1] for i in range(0, len(ones), 2)]
                twos = [twos[i] + twos[i + 1] for i in range(0, len(twos), 2)]
            one = ones[0].astype(jnp.float32)
            two = twos[0].astype(jnp.float32)
            re = re + (one[:half] + one[half:])
            im = im + (two[:half] + two[half:])
        return re, im

    def one_target(target, carry):
        zero = jnp.zeros((half, LANES), jnp.float32)
        acc = some_slots(target, 0, fixed, (zero, zero))
        more = count_ref[target]
        acc = lax.fori_loop(
            0, more, lambda i, acc: some_slots(target, fixed + i * chunk, chunk, acc), acc
        )
        sums[target, :half] = acc[0]
        sums[target, half:] = acc[1]
        return carry

    lax.fori_loop(0, src_ref.shape[0], one_target, 0)
    for part in range(2):
        pieces = [sums[:, part * half + i, :] for i in range(half)]
        whole = jnp.concatenate(pieces, 1)[:, :half_width]
        out_ref[:, part * half_width : (part + 1) * half_width] = whole.astype(out_ref.dtype)


def interact(table, sources, kinds, transfer, half_width):
    width = -(-half_width // LANES) * LANES
    targets, slots = sources.shape
    kinds_count = transfer.shape[0]
    fixed = -(-(slots // 2) // CHUNK) * CHUNK
    padded = fixed + -(-(slots - fixed) // CHUNK) * CHUNK
    live = sources >= 0
    tail = ((0, 0), (0, padded - slots))
    src = jnp.pad(jnp.where(live, sources, 0), tail)
    kind = jnp.pad(jnp.where(live, kinds, kinds_count), tail, constant_values=kinds_count)
    lengths = jnp.sum(live.astype(jnp.int32), 1)
    more = jnp.maximum(lengths - fixed + CHUNK - 1, 0) // CHUNK
    real, imag = transfer[:, :half_width], transfer[:, half_width:]
    ones = tiled(jnp.concatenate([real, -imag], 1), half_width, width)
    twos = tiled(jnp.concatenate([imag, real], 1), half_width, width)
    coef = jnp.pad(jnp.concatenate([ones, twos], 1), ((0, 1), (0, 0), (0, 0)))
    smem = pl.BlockSpec(memory_space=pltpu.SMEM)
    vmem = pl.BlockSpec(memory_space=pltpu.VMEM)
    return pl.pallas_call(
        functools.partial(interact_kernel, fixed, CHUNK, half_width),
        out_shape=jax.ShapeDtypeStruct((targets, 2 * half_width), jnp.bfloat16),
        in_specs=[smem, smem, smem, vmem, vmem],
        out_specs=vmem,
        scratch_shapes=[pltpu.VMEM((targets, table.shape[1], LANES), jnp.float32)],
        compiler_params=pltpu.CompilerParams(vmem_limit_bytes=24 * 2**20),
        name="interact",
    )(more, src, kind, table, coef)


def shards(
    leaf_spectra, leaf_keys, parent_keys, child_phase, coarsen, transfer, vlist_src, vlist_type
):
    half_width = child_phase.shape[1]
    child_code = leaf_keys % 8
    parent_of = leaf_keys // 8
    phase_table = jnp.concatenate([jnp.cos(child_phase), jnp.sin(child_phase)], 1)
    picker = (child_code[:, None] == jnp.arange(8, dtype=jnp.int32)[None, :]).astype(jnp.float32)
    factors = jnp.dot(picker, phase_table, precision=lax.Precision.HIGHEST)
    cosine = factors[:, :half_width]
    sine_part = factors[:, half_width:]
    spectra = leaf_spectra.astype(jnp.float32)
    real_in = spectra[:, :half_width]
    imag_in = spectra[:, half_width:]
    twisted = jnp.concatenate(
        [real_in * cosine - imag_in * sine_part, real_in * sine_part + imag_in * cosine], 1
    )
    membership = (parent_of[:, None] == parent_keys[None, :]).astype(jnp.float32)
    gathered = jnp.einsum("lp,lc->pc", membership, twisted, precision=lax.Precision.HIGHEST)
    tail_mask = (parent_of < parent_keys[0]).astype(jnp.float32)
    tail_sum = jnp.dot(tail_mask, twisted, precision=lax.Precision.HIGHEST)
    incoming = passed_along(tail_sum, "oct", -1)
    gathered = jnp.concatenate([gathered[:-1], gathered[-1:] + incoming[None, :]], 0)
    gathered_b = gathered.astype(jnp.bfloat16)
    real_b = gathered_b[:, :half_width]
    imag_b = gathered_b[:, half_width:]
    real_out = jnp.dot(real_b, coarsen[0], preferred_element_type=jnp.float32) - jnp.dot(
        imag_b, coarsen[1], preferred_element_type=jnp.float32
    )
    imag_out = jnp.dot(real_b, coarsen[1], preferred_element_type=jnp.float32) + jnp.dot(
        imag_b, coarsen[0], preferred_element_type=jnp.float32
    )
    upward = jnp.concatenate([real_out, imag_out], 1).astype(jnp.bfloat16)
    width = -(-half_width // LANES) * LANES
    own = tiled(upward, half_width, width)
    window_count = 2**GBITS
    blocks = [own]
    for distance in range(1, window_count):
        received = from_behind(own, "oct", distance)
        blocks = [received] + blocks
    table = jnp.concatenate(blocks, 0)
    local_field = interact(table, vlist_src, vlist_type, transfer, half_width)
    return (upward, local_field)


def solution(mesh):
    return jax.shard_map(
        shards,
        mesh=mesh,
        in_specs=(
            P("oct", None),
            P("oct"),
            P("oct"),
            P(),
            P(),
            P(),
            P("oct", None),
            P("oct", None),
        ),
        out_specs=(P("oct", None), P("oct", None)),
        check_vma=False,
    )
```

```python
import functools
import jax
import jax.numpy as jnp
from jax import lax
from jax.experimental import pallas as pl
from jax.experimental.pallas import tpu as pltpu
from jax.sharding import PartitionSpec as P

GBITS = 3
LANES = 128
CHUNK = 32
PARTS = 2


def passed_along(value, axis, steps):
    count = lax.axis_size(axis)
    first, last = (max(0, -steps), min(count, count - steps))
    return lax.ppermute(value, axis, [(source, source + steps) for source in range(first, last)])


def tiled(values, half_width, width):
    rows = values.shape[0]
    halves = values.reshape(rows, 2, half_width)
    halves = jnp.pad(halves, ((0, 0), (0, 0), (0, width - half_width)))
    return halves.reshape(rows, 2 * width // LANES, LANES)


def exchange_kernel(axis, count, group, own_ref, window_ref, prev_ref, *sems):
    z_send, z_recv, far_send, far_recv, near_send, near_recv, pass_send, pass_recv, own_sem = sems
    me = lax.axis_index(axis)
    r = lax.rem(me, group)
    base = me - r
    after = lax.rem(me + group, count)
    before = lax.rem(me + count - group, count)
    twin = me + 1 - 2 * lax.rem(r, 2)
    steps = range(2, group, 2)
    piece = own_ref.shape[0] // PARTS

    barrier = pltpu.get_barrier_semaphore()
    greeted = [after, before, twin] + [base + lax.rem(r + step, group) for step in steps]
    for device in greeted:
        pl.semaphore_signal(barrier, inc=1, device_id={axis: device}, device_id_type=pl.DeviceIdType.MESH)
    pl.semaphore_wait(barrier, len(greeted))

    def copy(source, target, send, recv, device):
        return pltpu.make_async_remote_copy(
            src_ref=source, dst_ref=target, send_sem=send, recv_sem=recv,
            device_id={axis: device}, device_id_type=pl.DeviceIdType.MESH,
        )

    def rows_of(part):
        return pl.ds(part * piece, piece)

    def along(part):
        return copy(own_ref.at[rows_of(part)], prev_ref.at[rows_of(part)], z_send.at[part], z_recv.at[part], after)

    def far(block, index, part):
        peer = base + lax.rem(r + steps[index], group)
        return copy(
            block.at[rows_of(part)], window_ref.at[r, rows_of(part)],
            far_send.at[index, part], far_recv.at[index, part], peer,
        )

    def near(block, part):
        return copy(
            block.at[rows_of(part)], window_ref.at[r, rows_of(part)], near_send.at[part], near_recv.at[part], twin
        )

    def onward(index, part):
        slot = lax.rem(r + group - steps[index], group)
        here = window_ref.at[slot, rows_of(part)]
        return copy(here, here, pass_send.at[index, part], pass_recv.at[index, part], twin)

    parts = range(PARTS)
    indices = range(len(steps))
    for part in parts:
        along(part).start()
    for part in parts:
        for index in indices:
            @pl.when(r + steps[index] < group)
            def _():
                far(own_ref, index, part).start()
    @pl.when(lax.rem(r, 2) == 0)
    def _():
        for part in parts:
            near(own_ref, part).start()
    own_copy = pltpu.make_async_copy(own_ref, window_ref.at[r], own_sem)
    own_copy.start()
    for part in parts:
        along(part).wait_recv()
        for index in indices:
            @pl.when(r + steps[index] >= group)
            def _():
                far(prev_ref, index, part).start()
        @pl.when(lax.rem(r, 2) == 1)
        def _():
            near(prev_ref, part).start()
    for index in indices:
        for part in parts:
            far(own_ref, index, part).wait_recv()
            onward(index, part).start()
    for part in parts:
        near(own_ref, part).wait_recv()
        for index in indices:
            onward(index, part).wait_recv()
    for part in parts:
        along(part).wait_send()
        near(own_ref, part).wait_send()
        for index in indices:
            far(own_ref, index, part).wait_send()
            onward(index, part).wait_send()
    own_copy.wait()


def exchange(own, axis, group):
    others = group // 2 - 1
    dma = pltpu.SemaphoreType.DMA
    anywhere = pl.BlockSpec(memory_space=pl.ANY)
    return pl.pallas_call(
        functools.partial(exchange_kernel, axis, lax.axis_size(axis), group),
        out_shape=[
            jax.ShapeDtypeStruct((group,) + own.shape, own.dtype),
            jax.ShapeDtypeStruct(own.shape, own.dtype),
        ],
        in_specs=[anywhere],
        out_specs=[anywhere, anywhere],
        scratch_shapes=[
            dma((PARTS,)), dma((PARTS,)),
            dma((others, PARTS)), dma((others, PARTS)),
            dma((PARTS,)), dma((PARTS,)),
            dma((others, PARTS)), dma((others, PARTS)),
            dma,
        ],
        compiler_params=pltpu.CompilerParams(collective_id=0, has_side_effects=True),
        name="exchange",
    )(own)[0]


def interact_kernel(
    fixed, chunk, half_width, count_ref, src_ref, kind_ref, window_ref, transfer_ref, out_ref, table, coef, sums
):
    rows = table.shape[1]
    half = rows // 2
    kinds = transfer_ref.shape[0]
    step = 16

    def widen(i, carry):
        part = pl.ds(pl.multiple_of(i * step, step), step)
        table[part] = window_ref[part].astype(jnp.float32)
        return carry

    lax.fori_loop(0, table.shape[0] // step, widen, 0)

    def lay_out(start, count):
        block = transfer_ref[pl.ds(start, count), :].astype(jnp.float32)
        for part in range(2):
            whole = block[:, part * half_width : (part + 1) * half_width]
            whole = jnp.concatenate([whole, jnp.zeros((count, half * LANES - half_width), jnp.float32)], 1)
            for i in range(half):
                coef[pl.ds(start, count), part * half + i, :] = whole[:, i * LANES : (i + 1) * LANES]

    def lay_out_step(i, carry):
        lay_out(pl.multiple_of(i * step, step), step)
        return carry

    even = kinds // step
    lax.fori_loop(0, even, lay_out_step, 0)
    if kinds % step:
        lay_out(even * step, kinds % step)
    coef[kinds] = jnp.zeros(coef.shape[1:], jnp.float32)

    def some_slots(target, first, count, acc):
        re, im = acc
        for slot in range(count):
            source = table[src_ref[target, first + slot]]
            factor = coef[kind_ref[target, first + slot]]
            re = re + (factor[:half] * source[:half] - factor[half:] * source[half:])
            im = im + (factor[:half] * source[half:] + factor[half:] * source[:half])
        return re, im

    def one_target(target, carry):
        zero = jnp.zeros((half, LANES), jnp.float32)
        acc = some_slots(target, 0, fixed, (zero, zero))
        more = count_ref[target]
        acc = lax.fori_loop(
            0, more, lambda i, acc: some_slots(target, fixed + i * chunk, chunk, acc), acc
        )
        sums[target, :half] = acc[0]
        sums[target, half:] = acc[1]
        return carry

    lax.fori_loop(0, src_ref.shape[0], one_target, 0)
    for part in range(2):
        pieces = [sums[:, part * half + i, :] for i in range(half)]
        whole = jnp.concatenate(pieces, 1)[:, :half_width]
        out_ref[:, part * half_width : (part + 1) * half_width] = whole.astype(out_ref.dtype)


def interact(window, sources, kinds, transfer, half_width):
    rows = window.shape[1]
    targets, slots = sources.shape
    kinds_count = transfer.shape[0]
    fixed = -(-(slots // 2) // CHUNK) * CHUNK
    padded = fixed + -(-(slots - fixed) // CHUNK) * CHUNK
    live = sources >= 0
    tail = ((0, 0), (0, padded - slots))
    src = jnp.pad(jnp.where(live, sources, 0), tail)
    kind = jnp.pad(jnp.where(live, kinds, kinds_count), tail, constant_values=kinds_count)
    lengths = jnp.sum(live.astype(jnp.int32), 1)
    more = jnp.maximum(lengths - fixed + CHUNK - 1, 0) // CHUNK
    smem = pl.BlockSpec(memory_space=pltpu.SMEM)
    vmem = pl.BlockSpec(memory_space=pltpu.VMEM)
    return pl.pallas_call(
        functools.partial(interact_kernel, fixed, CHUNK, half_width),
        out_shape=jax.ShapeDtypeStruct((targets, 2 * half_width), jnp.bfloat16),
        in_specs=[smem, smem, smem, vmem, vmem],
        out_specs=vmem,
        scratch_shapes=[
            pltpu.VMEM(window.shape, jnp.float32),
            pltpu.VMEM((kinds_count + 1, rows, LANES), jnp.float32),
            pltpu.VMEM((targets, rows, LANES), jnp.float32),
        ],
        compiler_params=pltpu.CompilerParams(vmem_limit_bytes=32 * 2**20),
        name="interact",
    )(more, src, kind, window, transfer)


def shards(
    leaf_spectra, leaf_keys, parent_keys, child_phase, coarsen, transfer, vlist_src, vlist_type
):
    half_width = child_phase.shape[1]
    child_code = leaf_keys % 8
    parent_of = leaf_keys // 8
    phase_table = jnp.concatenate([jnp.cos(child_phase), jnp.sin(child_phase)], 1)
    picker = (child_code[:, None] == jnp.arange(8, dtype=jnp.int32)[None, :]).astype(jnp.float32)
    factors = jnp.dot(picker, phase_table, precision=lax.Precision.HIGHEST)
    cosine = factors[:, :half_width]
    sine_part = factors[:, half_width:]
    spectra = leaf_spectra.astype(jnp.float32)
    real_in = spectra[:, :half_width]
    imag_in = spectra[:, half_width:]
    twisted = jnp.concatenate(
        [real_in * cosine - imag_in * sine_part, real_in * sine_part + imag_in * cosine], 1
    )
    membership = (parent_of[:, None] == parent_keys[None, :]).astype(jnp.float32)
    gathered = jnp.einsum("lp,lc->pc", membership, twisted, precision=lax.Precision.HIGHEST)
    tail_mask = (parent_of < parent_keys[0]).astype(jnp.float32)
    tail_sum = jnp.dot(tail_mask, twisted, precision=lax.Precision.HIGHEST)
    incoming = passed_along(tail_sum, "oct", -1)
    gathered = jnp.concatenate([gathered[:-1], gathered[-1:] + incoming[None, :]], 0)
    gathered_b = gathered.astype(jnp.bfloat16)
    real_b = gathered_b[:, :half_width]
    imag_b = gathered_b[:, half_width:]
    real_out = jnp.dot(real_b, coarsen[0], preferred_element_type=jnp.float32) - jnp.dot(
        imag_b, coarsen[1], preferred_element_type=jnp.float32
    )
    imag_out = jnp.dot(real_b, coarsen[1], preferred_element_type=jnp.float32) + jnp.dot(
        imag_b, coarsen[0], preferred_element_type=jnp.float32
    )
    upward = jnp.concatenate([real_out, imag_out], 1).astype(jnp.bfloat16)
    width = -(-half_width // LANES) * LANES
    own = tiled(upward, half_width, width)
    group = 2**GBITS
    rows = own.shape[0]
    window = exchange(own, "oct", group).reshape((group * rows,) + own.shape[1:])
    rank = lax.rem(lax.axis_index("oct"), group)
    slot = (vlist_src // rows + rank + 1) % group
    sources = jnp.where(vlist_src >= 0, slot * rows + vlist_src % rows, -1)
    local_field = interact(window, sources, vlist_type, transfer, half_width)
    return (upward, local_field)


def solution(mesh):
    return jax.shard_map(
        shards,
        mesh=mesh,
        in_specs=(
            P("oct", None),
            P("oct"),
            P("oct"),
            P(),
            P(),
            P(),
            P("oct", None),
            P("oct", None),
        ),
        out_specs=(P("oct", None), P("oct", None)),
        check_vma=False,
    )
```

```python
import functools
import jax
import jax.numpy as jnp
from jax import lax
from jax.experimental import pallas as pl
from jax.experimental.pallas import tpu as pltpu
from jax.sharding import PartitionSpec as P

GBITS = 3
LANES = 128
CHUNK = 16
PARTS = 4


def upward_kernel(
    axis, count, group, keys_ref, wanted_ref, phase_ref, leaf_ref, coarsen_ref, up_ref, window_ref, prev_ref,
    coarsen_here, tail_out, tail_in, own_wide, own_ref, *sems
):
    (z_send, z_recv, far_send, far_recv, near_send, near_recv, pass_send, pass_recv,
     own_sem, coarsen_sem, tail_send, tail_recv) = sems
    coarsen_copy = pltpu.make_async_copy(coarsen_ref, coarsen_here, coarsen_sem)
    coarsen_copy.start()
    me = lax.axis_index(axis)
    r = lax.rem(me, group)
    base = me - r
    after = lax.rem(me + group, count)
    before = lax.rem(me + count - group, count)
    twin = me + 1 - 2 * lax.rem(r, 2)
    steps = range(2, group, 2)
    piece = own_ref.shape[0] // PARTS

    barrier = pltpu.get_barrier_semaphore()
    left, right = lax.rem(me + count - 1, count), lax.rem(me + 1, count)
    greeted = [after, before, twin, left, right] + [base + lax.rem(r + step, group) for step in steps]
    for device in greeted:
        pl.semaphore_signal(barrier, inc=1, device_id={axis: device}, device_id_type=pl.DeviceIdType.MESH)
    pl.semaphore_wait(barrier, len(greeted))

    def copy(source, target, send, recv, device):
        return pltpu.make_async_remote_copy(
            src_ref=source, dst_ref=target, send_sem=send, recv_sem=recv,
            device_id={axis: device}, device_id_type=pl.DeviceIdType.MESH,
        )

    def rows_of(part):
        return pl.ds(part * piece, piece)

    def along(part):
        return copy(own_ref.at[rows_of(part)], prev_ref.at[rows_of(part)], z_send.at[part], z_recv.at[part], after)

    def far(block, index, part):
        peer = base + lax.rem(r + steps[index], group)
        return copy(
            block.at[rows_of(part)], window_ref.at[r, rows_of(part)],
            far_send.at[index, part], far_recv.at[index, part], peer,
        )

    def near(block, part):
        return copy(
            block.at[rows_of(part)], window_ref.at[r, rows_of(part)], near_send.at[part], near_recv.at[part], twin
        )

    def onward(index, part):
        slot = lax.rem(r + group - steps[index], group)
        here = window_ref.at[slot, rows_of(part)]
        return copy(here, here, pass_send.at[index, part], pass_recv.at[index, part], twin)

    half_width = phase_ref.shape[1]
    codes = phase_ref.shape[0]
    rows = own_ref.shape[0]
    cosine, sine = jnp.cos(phase_ref[...]), jnp.sin(phase_ref[...])
    keys = keys_ref[...]
    real_in, imag_in = leaf_ref[:, :half_width], leaf_ref[:, half_width:]

    def selected(mask):
        picker = jnp.where(mask, 1.0, 0.0).astype(jnp.bfloat16)
        real = jnp.dot(picker, real_in, preferred_element_type=jnp.float32)
        return real, jnp.dot(picker, imag_in, preferred_element_type=jnp.float32)

    code = lax.broadcasted_iota(jnp.int32, (codes, keys.shape[1]), 0)
    real, imag = selected(((keys & (codes - 1)) == code) & (keys < wanted_ref[0:1, :]))
    tail_out[0:1, :half_width] = jnp.sum(real * cosine - imag * sine, 0, keepdims=True)
    tail_out[1:2, :half_width] = jnp.sum(real * sine + imag * cosine, 0, keepdims=True)
    tail_copy = copy(tail_out, tail_in, tail_send, tail_recv, left)
    tail_copy.start()

    real, imag = selected(wanted_ref[...] == keys)
    real_sum = jnp.zeros((rows, half_width), jnp.float32)
    imag_sum = jnp.zeros((rows, half_width), jnp.float32)
    for c in range(codes):
        a, b = real[c * rows : (c + 1) * rows], imag[c * rows : (c + 1) * rows]
        real_sum = real_sum + (a * cosine[c : c + 1] - b * sine[c : c + 1])
        imag_sum = imag_sum + (a * sine[c : c + 1] + b * cosine[c : c + 1])
    tail_copy.wait_recv()
    last = lax.broadcasted_iota(jnp.int32, (rows, 1), 0) == rows - 1
    real_sum = real_sum + jnp.where(last, tail_in[0:1, :half_width], 0.0)
    imag_sum = imag_sum + jnp.where(last, tail_in[1:2, :half_width], 0.0)
    gathered = jnp.concatenate([real_sum, imag_sum], 0).astype(jnp.bfloat16)
    coarsen_copy.wait()
    by_real = jnp.dot(gathered, coarsen_here[0], preferred_element_type=jnp.float32)
    by_imag = jnp.dot(gathered, coarsen_here[1], preferred_element_type=jnp.float32)
    outs = (by_real[:rows] - by_imag[rows:], by_imag[:rows] + by_real[rows:])
    tiles = own_wide.shape[1] // 2
    padding = jnp.zeros((rows, tiles * LANES - half_width), jnp.float32)
    for part in range(2):
        whole = jnp.concatenate([outs[part], padding], 1)
        for i in range(tiles):
            own_wide[:, part * tiles + i, :] = whole[:, i * LANES : (i + 1) * LANES]
    own_ref[...] = own_wide[...].astype(own_ref.dtype)

    parts = range(PARTS)
    indices = range(len(steps))
    @pl.when(r > 0)
    def _():
        for part in parts:
            along(part).start()
    for part in parts:
        for index in indices:
            @pl.when(r + steps[index] < group)
            def _():
                far(own_ref, index, part).start()
    @pl.when(lax.rem(r, 2) == 0)
    def _():
        for part in parts:
            near(own_ref, part).start()
    own_copy = pltpu.make_async_copy(own_ref, window_ref.at[r], own_sem)
    own_copy.start()
    for part in range(2):
        up_ref[:, part * half_width : (part + 1) * half_width] = outs[part].astype(up_ref.dtype)
    for part in parts:
        @pl.when(r > 0)
        def _():
            along(part).wait_recv()
        for index in indices:
            @pl.when(r + steps[index] >= group)
            def _():
                far(prev_ref, index, part).start()
        @pl.when(lax.rem(r, 2) == 1)
        def _():
            near(prev_ref, part).start()
    for index in indices:
        for part in parts:
            far(own_ref, index, part).wait_recv()
            onward(index, part).start()
    for part in parts:
        near(own_ref, part).wait_recv()
        for index in indices:
            onward(index, part).wait_recv()
    tail_copy.wait_send()
    for part in parts:
        @pl.when(r > 0)
        def _():
            along(part).wait_send()
        near(own_ref, part).wait_send()
        for index in indices:
            far(own_ref, index, part).wait_send()
            onward(index, part).wait_send()
    own_copy.wait()


def upward_and_window(leaf_spectra, leaf_keys, parent_keys, child_phase, coarsen, axis, group):
    half_width = child_phase.shape[1]
    rows = parent_keys.shape[0]
    codes = child_phase.shape[0]
    tiles = 2 * (-(-half_width // LANES))
    wanted = (jnp.arange(codes, dtype=jnp.int32)[:, None] + codes * parent_keys[None, :]).reshape(-1, 1)
    others = group // 2 - 1
    dma = pltpu.SemaphoreType.DMA
    anywhere = pl.BlockSpec(memory_space=pl.ANY)
    vmem = pl.BlockSpec(memory_space=pltpu.VMEM)
    own = (rows, tiles, LANES)
    upward, window, _ = pl.pallas_call(
        functools.partial(upward_kernel, axis, lax.axis_size(axis), group),
        out_shape=[
            jax.ShapeDtypeStruct((rows, 2 * half_width), jnp.bfloat16),
            jax.ShapeDtypeStruct((group,) + own, jnp.bfloat16),
            jax.ShapeDtypeStruct(own, jnp.bfloat16),
        ],
        in_specs=[vmem, vmem, vmem, vmem, anywhere],
        out_specs=[vmem, anywhere, anywhere],
        scratch_shapes=[
            pltpu.VMEM(coarsen.shape, coarsen.dtype),
            pltpu.VMEM((2, tiles // 2 * LANES), jnp.float32),
            pltpu.VMEM((2, tiles // 2 * LANES), jnp.float32),
            pltpu.VMEM(own, jnp.float32),
            pltpu.VMEM(own, jnp.bfloat16),
            dma((PARTS,)), dma((PARTS,)),
            dma((others, PARTS)), dma((others, PARTS)),
            dma((PARTS,)), dma((PARTS,)),
            dma((others, PARTS)), dma((others, PARTS)),
            dma, dma, dma, dma,
        ],
        compiler_params=pltpu.CompilerParams(
            collective_id=0, has_side_effects=True, vmem_limit_bytes=32 * 2**20
        ),
        name="upward_and_window",
    )(leaf_keys.reshape(1, -1), wanted, child_phase, leaf_spectra, coarsen)
    return upward, window


def interact_kernel(
    fixed, chunk, half_width, count_ref, src_ref, kind_ref, window_ref, transfer_ref, out_ref, table, coef, sums,
    window_here, window_sem
):
    rows = table.shape[1]
    half = rows // 2
    kinds = transfer_ref.shape[0]
    step = 16

    window_copy = pltpu.make_async_copy(window_ref, window_here, window_sem)
    window_copy.start()

    def widen(i, carry):
        part = pl.ds(pl.multiple_of(i * step, step), step)
        table[part] = window_here[part].astype(jnp.float32)
        return carry

    def lay_out(start, count):
        block = transfer_ref[pl.ds(start, count), :].astype(jnp.float32)
        for part in range(2):
            whole = block[:, part * half_width : (part + 1) * half_width]
            whole = jnp.concatenate([whole, jnp.zeros((count, half * LANES - half_width), jnp.float32)], 1)
            for i in range(half):
                coef[pl.ds(start, count), part * half + i, :] = whole[:, i * LANES : (i + 1) * LANES]

    def lay_out_step(i, carry):
        lay_out(pl.multiple_of(i * step, step), step)
        return carry

    even = kinds // step
    lax.fori_loop(0, even, lay_out_step, 0)
    if kinds % step:
        lay_out(even * step, kinds % step)
    coef[kinds] = jnp.zeros(coef.shape[1:], jnp.float32)
    window_copy.wait()
    lax.fori_loop(0, table.shape[0] // step, widen, 0)

    def some_slots(target, first, count, acc):
        re, im = acc
        for slot in range(count):
            source = table[src_ref[target, first + slot]]
            factor = coef[kind_ref[target, first + slot]]
            re = re + (factor[:half] * source[:half] - factor[half:] * source[half:])
            im = im + (factor[:half] * source[half:] + factor[half:] * source[:half])
        return re, im

    most = (src_ref.shape[1] - fixed) // chunk

    def one_target(target, carry):
        def exactly(chunks):
            zero = jnp.zeros((half, LANES), jnp.float32)
            acc = some_slots(target, 0, fixed + chunks * chunk, (zero, zero))
            sums[target, :half] = acc[0]
            sums[target, half:] = acc[1]

        def between(low, high):
            if low == high:
                exactly(low)
                return
            middle = (low + high) // 2
            lax.cond(more <= middle, lambda: between(low, middle), lambda: between(middle + 1, high))

        more = count_ref[target]
        between(0, most)
        return carry

    lax.fori_loop(0, src_ref.shape[0], one_target, 0)
    for part in range(2):
        pieces = [sums[:, part * half + i, :] for i in range(half)]
        whole = jnp.concatenate(pieces, 1)[:, :half_width]
        out_ref[:, part * half_width : (part + 1) * half_width] = whole.astype(out_ref.dtype)


def interact(window, sources, kinds, transfer, half_width):
    rows = window.shape[1]
    targets, slots = sources.shape
    kinds_count = transfer.shape[0]
    fixed = -(-(slots // 2) // CHUNK) * CHUNK
    padded = fixed + -(-(slots - fixed) // CHUNK) * CHUNK
    live = sources >= 0
    tail = ((0, 0), (0, padded - slots))
    src = jnp.pad(jnp.where(live, sources, 0), tail)
    kind = jnp.pad(jnp.where(live, kinds, kinds_count), tail, constant_values=kinds_count)
    lengths = jnp.sum(live.astype(jnp.int32), 1)
    more = jnp.maximum(lengths - fixed + CHUNK - 1, 0) // CHUNK
    smem = pl.BlockSpec(memory_space=pltpu.SMEM)
    vmem = pl.BlockSpec(memory_space=pltpu.VMEM)
    return pl.pallas_call(
        functools.partial(interact_kernel, fixed, CHUNK, half_width),
        out_shape=jax.ShapeDtypeStruct((targets, 2 * half_width), jnp.bfloat16),
        in_specs=[smem, smem, smem, pl.BlockSpec(memory_space=pl.ANY), vmem],
        out_specs=vmem,
        scratch_shapes=[
            pltpu.VMEM(window.shape, jnp.float32),
            pltpu.VMEM((kinds_count + 1, rows, LANES), jnp.float32),
            pltpu.VMEM((targets, rows, LANES), jnp.float32),
            pltpu.VMEM(window.shape, window.dtype),
            pltpu.SemaphoreType.DMA,
        ],
        compiler_params=pltpu.CompilerParams(vmem_limit_bytes=32 * 2**20),
        name="interact",
    )(more, src, kind, window, transfer)


def shards(
    leaf_spectra, leaf_keys, parent_keys, child_phase, coarsen, transfer, vlist_src, vlist_type
):
    half_width = child_phase.shape[1]
    group = 2**GBITS
    upward, window = upward_and_window(
        leaf_spectra, leaf_keys, parent_keys, child_phase, coarsen, "oct", group
    )
    rows = parent_keys.shape[0]
    window = window.reshape((group * rows,) + window.shape[2:])
    rank = lax.rem(lax.axis_index("oct"), group)
    slot = (vlist_src // rows + rank + 1) % group
    sources = jnp.where(vlist_src >= 0, slot * rows + vlist_src % rows, -1)
    local_field = interact(window, sources, vlist_type, transfer, half_width)
    return (upward, local_field)


def solution(mesh):
    return jax.shard_map(
        shards,
        mesh=mesh,
        in_specs=(
            P("oct", None),
            P("oct"),
            P("oct"),
            P(),
            P(),
            P(),
            P("oct", None),
            P("oct", None),
        ),
        out_specs=(P("oct", None), P("oct", None)),
        check_vma=False,
    )
```

```python
import functools
import jax
import jax.numpy as jnp
from jax import lax
from jax.experimental import pallas as pl
from jax.experimental.pallas import tpu as pltpu
from jax.sharding import PartitionSpec as P

GBITS = 3
LANES = 128
CHUNK = 16
PARTS = 4


def upward_kernel(
    axis, count, group, fixed, chunk, keys_ref, wanted_ref, phase_ref, vsrc_ref, vtype_ref, leaf_hbm, coarsen_hbm,
    transfer_hbm, up_ref, window_ref, prev_ref, coef_hbm, src_ref, kind_ref, more_ref,
    leaf_ref, coarsen_ref, transfer_ref, tail_out, tail_in, own_wide, own_ref, coef_wide, coef, *sems
):
    (z_send, z_recv, far_send, far_recv, near_send, near_recv, pass_send, pass_recv,
     own_sem, leaf_sem, coarsen_sem, transfer_sem, coef_sem, tail_send, tail_recv) = sems
    leaf_copy = pltpu.make_async_copy(leaf_hbm, leaf_ref, leaf_sem)
    leaf_copy.start()
    coarsen_copy = pltpu.make_async_copy(coarsen_hbm, coarsen_ref, coarsen_sem)
    coarsen_copy.start()
    transfer_copy = pltpu.make_async_copy(transfer_hbm, transfer_ref, transfer_sem)
    transfer_copy.start()
    me = lax.axis_index(axis)
    r = lax.rem(me, group)
    base = me - r
    after = lax.rem(me + group, count)
    before = lax.rem(me + count - group, count)
    twin = me + 1 - 2 * lax.rem(r, 2)
    steps = range(2, group, 2)
    piece = own_ref.shape[0] // PARTS

    barrier = pltpu.get_barrier_semaphore()
    left, right = lax.rem(me + count - 1, count), lax.rem(me + 1, count)
    greeted = [after, before, twin, left, right] + [base + lax.rem(r + step, group) for step in steps]
    for device in greeted:
        pl.semaphore_signal(barrier, inc=1, device_id={axis: device}, device_id_type=pl.DeviceIdType.MESH)
    pl.semaphore_wait(barrier, len(greeted))

    def copy(source, target, send, recv, device):
        return pltpu.make_async_remote_copy(
            src_ref=source, dst_ref=target, send_sem=send, recv_sem=recv,
            device_id={axis: device}, device_id_type=pl.DeviceIdType.MESH,
        )

    def rows_of(part):
        return pl.ds(part * piece, piece)

    def along(part):
        return copy(own_ref.at[rows_of(part)], prev_ref.at[rows_of(part)], z_send.at[part], z_recv.at[part], after)

    def far(block, index, part):
        peer = base + lax.rem(r + steps[index], group)
        return copy(
            block.at[rows_of(part)], window_ref.at[r, rows_of(part)],
            far_send.at[index, part], far_recv.at[index, part], peer,
        )

    def near(block, part):
        return copy(
            block.at[rows_of(part)], window_ref.at[r, rows_of(part)], near_send.at[part], near_recv.at[part], twin
        )

    def onward(index, part):
        slot = lax.rem(r + group - steps[index], group)
        here = window_ref.at[slot, rows_of(part)]
        return copy(here, here, pass_send.at[index, part], pass_recv.at[index, part], twin)

    half_width = phase_ref.shape[1]
    codes = phase_ref.shape[0]
    rows = own_ref.shape[0]
    cosine, sine = jnp.cos(phase_ref[...]), jnp.sin(phase_ref[...])
    keys = keys_ref[...]
    leaf_copy.wait()
    real_in, imag_in = leaf_ref[:, :half_width], leaf_ref[:, half_width:]

    def selected(mask):
        picker = jnp.where(mask, 1.0, 0.0).astype(jnp.bfloat16)
        real = jnp.dot(picker, real_in, preferred_element_type=jnp.float32)
        return real, jnp.dot(picker, imag_in, preferred_element_type=jnp.float32)

    code = lax.broadcasted_iota(jnp.int32, (codes, keys.shape[1]), 0)
    real, imag = selected(((keys & (codes - 1)) == code) & (keys < wanted_ref[0:1, :]))
    tail_out[0:1, :half_width] = jnp.sum(real * cosine - imag * sine, 0, keepdims=True)
    tail_out[1:2, :half_width] = jnp.sum(real * sine + imag * cosine, 0, keepdims=True)
    tail_copy = copy(tail_out, tail_in, tail_send, tail_recv, left)
    tail_copy.start()

    real, imag = selected(wanted_ref[...] == keys)
    real_sum = jnp.zeros((rows, half_width), jnp.float32)
    imag_sum = jnp.zeros((rows, half_width), jnp.float32)
    for c in range(codes):
        a, b = real[c * rows : (c + 1) * rows], imag[c * rows : (c + 1) * rows]
        real_sum = real_sum + (a * cosine[c : c + 1] - b * sine[c : c + 1])
        imag_sum = imag_sum + (a * sine[c : c + 1] + b * cosine[c : c + 1])
    tail_copy.wait_recv()
    last = lax.broadcasted_iota(jnp.int32, (rows, 1), 0) == rows - 1
    real_sum = real_sum + jnp.where(last, tail_in[0:1, :half_width], 0.0)
    imag_sum = imag_sum + jnp.where(last, tail_in[1:2, :half_width], 0.0)
    gathered = jnp.concatenate([real_sum, imag_sum], 0).astype(jnp.bfloat16)
    coarsen_copy.wait()
    by_real = jnp.dot(gathered, coarsen_ref[0], preferred_element_type=jnp.float32)
    by_imag = jnp.dot(gathered, coarsen_ref[1], preferred_element_type=jnp.float32)
    outs = (by_real[:rows] - by_imag[rows:], by_imag[:rows] + by_real[rows:])
    tiles = own_wide.shape[1] // 2
    padding = jnp.zeros((rows, tiles * LANES - half_width), jnp.float32)
    for part in range(2):
        whole = jnp.concatenate([outs[part], padding], 1)
        for i in range(tiles):
            own_wide[:, part * tiles + i, :] = whole[:, i * LANES : (i + 1) * LANES]
    own_ref[...] = own_wide[...].astype(own_ref.dtype)

    parts = range(PARTS)
    indices = range(len(steps))
    @pl.when(r > 0)
    def _():
        for part in parts:
            along(part).start()
    for part in parts:
        for index in indices:
            @pl.when(r + steps[index] < group)
            def _():
                far(own_ref, index, part).start()
    @pl.when(lax.rem(r, 2) == 0)
    def _():
        for part in parts:
            near(own_ref, part).start()
    own_copy = pltpu.make_async_copy(own_ref, window_ref.at[r], own_sem)
    own_copy.start()
    for part in range(2):
        up_ref[:, part * half_width : (part + 1) * half_width] = outs[part].astype(up_ref.dtype)

    transfer_copy.wait()
    kinds = transfer_ref.shape[0]
    step = coef_wide.shape[0]

    def lay_out(start, size):
        block = transfer_ref[pl.ds(start, size), :].astype(jnp.float32)
        padding = jnp.zeros((size, tiles * LANES - half_width), jnp.float32)
        for part in range(2):
            whole = jnp.concatenate([block[:, part * half_width : (part + 1) * half_width], padding], 1)
            for i in range(tiles):
                coef_wide[pl.ds(0, size), part * tiles + i, :] = whole[:, i * LANES : (i + 1) * LANES]
        coef[pl.ds(start, size)] = coef_wide[pl.ds(0, size)].astype(coef.dtype)

    def lay_out_step(i, carry):
        lay_out(pl.multiple_of(i * step, step), step)
        return carry

    lax.fori_loop(0, kinds // step, lay_out_step, 0)
    if kinds % step:
        lay_out(kinds // step * step, kinds % step)
    coef[kinds] = jnp.zeros(coef.shape[1:], coef.dtype)
    coef_copy = pltpu.make_async_copy(coef, coef_hbm, coef_sem)
    coef_copy.start()

    sources = vsrc_ref[...]
    slots = sources.shape[1]
    live = sources >= 0
    place = lax.rem(lax.div(sources, rows) + r + 1, group)
    src_ref[...] = jnp.zeros(src_ref.shape, jnp.int32)
    src_ref[:, :slots] = jnp.where(live, place * rows + lax.rem(sources, rows), 0)
    kind_ref[...] = jnp.full(kind_ref.shape, kinds, jnp.int32)
    kind_ref[:, :slots] = jnp.where(live, vtype_ref[...], kinds)
    lengths = jnp.sum(jnp.where(live, 1.0, 0.0), 1, keepdims=True).astype(jnp.int32)
    more_ref[...] = lax.div(jnp.maximum(lengths - fixed + chunk - 1, 0), chunk)
    for part in parts:
        @pl.when(r > 0)
        def _():
            along(part).wait_recv()
        for index in indices:
            @pl.when(r + steps[index] >= group)
            def _():
                far(prev_ref, index, part).start()
        @pl.when(lax.rem(r, 2) == 1)
        def _():
            near(prev_ref, part).start()
    for index in indices:
        for part in parts:
            far(own_ref, index, part).wait_recv()
            onward(index, part).start()
    for part in parts:
        near(own_ref, part).wait_recv()
        for index in indices:
            onward(index, part).wait_recv()
    coef_copy.wait()
    tail_copy.wait_send()
    for part in parts:
        @pl.when(r > 0)
        def _():
            along(part).wait_send()
        near(own_ref, part).wait_send()
        for index in indices:
            far(own_ref, index, part).wait_send()
            onward(index, part).wait_send()
    own_copy.wait()


def upward_and_window(
    leaf_spectra, leaf_keys, parent_keys, child_phase, coarsen, transfer, vlist_src, vlist_type, axis, group
):
    half_width = child_phase.shape[1]
    rows = parent_keys.shape[0]
    codes = child_phase.shape[0]
    tiles = 2 * (-(-half_width // LANES))
    wanted = (jnp.arange(codes, dtype=jnp.int32)[:, None] + codes * parent_keys[None, :]).reshape(-1, 1)
    slots = vlist_src.shape[1]
    fixed = slots // 2 // CHUNK * CHUNK
    padded = -(-slots // CHUNK) * CHUNK
    others = group // 2 - 1
    dma = pltpu.SemaphoreType.DMA
    anywhere = pl.BlockSpec(memory_space=pl.ANY)
    vmem = pl.BlockSpec(memory_space=pltpu.VMEM)
    own = (rows, tiles, LANES)
    coef = (transfer.shape[0] + 1, tiles, LANES)
    upward, window, _, coef, src, kind, more = pl.pallas_call(
        functools.partial(upward_kernel, axis, lax.axis_size(axis), group, fixed, CHUNK),
        out_shape=[
            jax.ShapeDtypeStruct((rows, 2 * half_width), jnp.bfloat16),
            jax.ShapeDtypeStruct((group,) + own, jnp.bfloat16),
            jax.ShapeDtypeStruct(own, jnp.bfloat16),
            jax.ShapeDtypeStruct(coef, jnp.bfloat16),
            jax.ShapeDtypeStruct((rows, padded), jnp.int32),
            jax.ShapeDtypeStruct((rows, padded), jnp.int32),
            jax.ShapeDtypeStruct((rows, 1), jnp.int32),
        ],
        in_specs=[vmem] * 5 + [anywhere] * 3,
        out_specs=[vmem, anywhere, anywhere, anywhere, vmem, vmem, vmem],
        scratch_shapes=[
            pltpu.VMEM(leaf_spectra.shape, leaf_spectra.dtype),
            pltpu.VMEM(coarsen.shape, coarsen.dtype),
            pltpu.VMEM(transfer.shape, transfer.dtype),
            pltpu.VMEM((2, tiles // 2 * LANES), jnp.float32),
            pltpu.VMEM((2, tiles // 2 * LANES), jnp.float32),
            pltpu.VMEM(own, jnp.float32),
            pltpu.VMEM(own, jnp.bfloat16),
            pltpu.VMEM((16, tiles, LANES), jnp.float32),
            pltpu.VMEM(coef, jnp.bfloat16),
            dma((PARTS,)), dma((PARTS,)),
            dma((others, PARTS)), dma((others, PARTS)),
            dma((PARTS,)), dma((PARTS,)),
            dma((others, PARTS)), dma((others, PARTS)),
            dma, dma, dma, dma, dma, dma, dma,
        ],
        compiler_params=pltpu.CompilerParams(
            collective_id=0, has_side_effects=True, vmem_limit_bytes=56 * 2**20
        ),
        name="upward_and_window",
    )(
        leaf_keys.reshape(1, -1), wanted, child_phase, vlist_src, vlist_type, leaf_spectra, coarsen, transfer
    )
    return upward, window, coef, src, kind, more, fixed


def interact_kernel(fixed, chunk, half_width, count_ref, src_ref, kind_ref, table, coef, out_ref, sums):
    rows = table.shape[1]
    half = rows // 2
    most = (src_ref.shape[1] - fixed) // chunk

    def some_slots(target, count):
        re = jnp.zeros((half, LANES), jnp.float32)
        im = jnp.zeros((half, LANES), jnp.float32)
        for slot in range(count):
            source = table[src_ref[target, slot]].astype(jnp.float32)
            factor = coef[kind_ref[target, slot]].astype(jnp.float32)
            re = re + (factor[:half] * source[:half] - factor[half:] * source[half:])
            im = im + (factor[:half] * source[half:] + factor[half:] * source[:half])
        sums[target, :half] = re
        sums[target, half:] = im

    def one_target(target, carry):
        def between(low, high):
            if low == high:
                some_slots(target, fixed + low * chunk)
                return
            middle = (low + high) // 2
            lax.cond(more <= middle, lambda: between(low, middle), lambda: between(middle + 1, high))

        more = count_ref[target, 0]
        between(0, most)
        return carry

    lax.fori_loop(0, src_ref.shape[0], one_target, 0)
    for part in range(2):
        pieces = [sums[:, part * half + i, :] for i in range(half)]
        whole = jnp.concatenate(pieces, 1)[:, :half_width]
        out_ref[:, part * half_width : (part + 1) * half_width] = whole.astype(out_ref.dtype)


def interact(window, coef, src, kind, more, fixed, half_width):
    targets = src.shape[0]
    smem = pl.BlockSpec(memory_space=pltpu.SMEM)
    vmem = pl.BlockSpec(memory_space=pltpu.VMEM)
    return pl.pallas_call(
        functools.partial(interact_kernel, fixed, CHUNK, half_width),
        out_shape=jax.ShapeDtypeStruct((targets, 2 * half_width), jnp.bfloat16),
        in_specs=[smem, smem, smem, vmem, vmem],
        out_specs=vmem,
        scratch_shapes=[pltpu.VMEM((targets, window.shape[1], LANES), jnp.float32)],
        compiler_params=pltpu.CompilerParams(vmem_limit_bytes=56 * 2**20),
        name="interact",
    )(more, src, kind, window, coef)


def shards(
    leaf_spectra, leaf_keys, parent_keys, child_phase, coarsen, transfer, vlist_src, vlist_type
):
    half_width = child_phase.shape[1]
    group = 2**GBITS
    upward, window, coef, src, kind, more, fixed = upward_and_window(
        leaf_spectra, leaf_keys, parent_keys, child_phase, coarsen, transfer, vlist_src, vlist_type, "oct", group
    )
    rows = parent_keys.shape[0]
    window = window.reshape((group * rows,) + window.shape[2:])
    local_field = interact(window, coef, src, kind, more, fixed, half_width)
    return (upward, local_field)


def solution(mesh):
    return jax.shard_map(
        shards,
        mesh=mesh,
        in_specs=(
            P("oct", None),
            P("oct"),
            P("oct"),
            P(),
            P(),
            P(),
            P("oct", None),
            P("oct", None),
        ),
        out_specs=(P("oct", None), P("oct", None)),
        check_vma=False,
    )
```

```python
import functools
import jax
import jax.numpy as jnp
from jax import lax
from jax.experimental import pallas as pl
from jax.experimental.pallas import tpu as pltpu
from jax.sharding import PartitionSpec as P

GBITS = 3
LANES = 128
CHUNK = 16
PARTS = 4
CHAINS = 4


def upward_kernel(
    axis, count, group, fixed, chunk, keys_ref, parents_ref, phase_ref, vsrc_ref, vtype_ref, leaf_hbm, coarsen_hbm,
    transfer_hbm, up_ref, window_ref, prev_ref, coef_hbm, src_ref, kind_ref, more_ref,
    leaf_ref, coarsen_ref, transfer_ref, tail_out, tail_in, own_wide, own_ref, coef_wide, coef, *sems
):
    (z_send, z_recv, far_send, far_recv, near_send, near_recv, pass_send, pass_recv,
     across_send, across_recv, own_sem, leaf_sem, coarsen_sem, transfer_sem, coef_sem, tail_send, tail_recv) = sems
    leaf_copy = pltpu.make_async_copy(leaf_hbm, leaf_ref, leaf_sem)
    leaf_copy.start()
    coarsen_copy = pltpu.make_async_copy(coarsen_hbm, coarsen_ref, coarsen_sem)
    coarsen_copy.start()
    transfer_copy = pltpu.make_async_copy(transfer_hbm, transfer_ref, transfer_sem)
    transfer_copy.start()
    me = lax.axis_index(axis)
    r = lax.rem(me, group)
    base = me - r
    after = lax.rem(me + group, count)
    before = lax.rem(me + count - group, count)
    twin = me + 1 - 2 * lax.rem(r, 2)
    core = lax.rem(r, 2)
    chip = lax.div(r, 2)
    flip_low = r + 2 - 4 * lax.rem(chip, 2)
    flip_high = r + 4 - 8 * lax.div(chip, 2)
    flip_both = flip_low + flip_high - r
    peers = (flip_low, flip_high)
    is_one = jnp.where(chip == 1, 1, 0)
    is_two = jnp.where(chip == 2, 1, 0)
    first = 1 - is_one
    passed = 2 * (2 - 2 * is_one - 2 * is_two - lax.div(chip, 3) + 3 * (is_one * core + is_two * (1 - core))) + core
    late = is_one * core + is_two * (1 - core)
    piece = own_ref.shape[0] // PARTS

    barrier = pltpu.get_barrier_semaphore()
    left, right = lax.rem(me + count - 1, count), lax.rem(me + 1, count)
    greeted = [after, before, twin, left, right] + [base + peer for peer in peers]
    for device in greeted:
        pl.semaphore_signal(barrier, inc=1, device_id={axis: device}, device_id_type=pl.DeviceIdType.MESH)
    pl.semaphore_wait(barrier, len(greeted))

    def copy(source, target, send, recv, device):
        return pltpu.make_async_remote_copy(
            src_ref=source, dst_ref=target, send_sem=send, recv_sem=recv,
            device_id={axis: device}, device_id_type=pl.DeviceIdType.MESH,
        )

    def rows_of(part):
        return pl.ds(part * piece, piece)

    def along(part):
        return copy(own_ref.at[rows_of(part)], prev_ref.at[rows_of(part)], z_send.at[part], z_recv.at[part], after)

    def far(block, index, part):
        return copy(
            block.at[rows_of(part)], window_ref.at[r, rows_of(part)],
            far_send.at[index, part], far_recv.at[index, part], base + peers[index],
        )

    def near(block, part):
        return copy(
            block.at[rows_of(part)], window_ref.at[r, rows_of(part)], near_send.at[part], near_recv.at[part], twin
        )

    def arrived(index, slot, part):
        here = window_ref.at[slot, rows_of(part)]
        return copy(here, here, far_send.at[0, part], far_recv.at[index, part], twin)

    def across(part):
        here = window_ref.at[passed, rows_of(part)]
        there = base + 2 * (3 - lax.div(passed, 2)) + core
        return copy(here, here, across_send.at[part], across_recv.at[part], there)

    def onward(index, slot, part):
        here = window_ref.at[slot, rows_of(part)]
        return copy(here, here, pass_send.at[index, part], pass_recv.at[index, part], twin)

    half_width = phase_ref.shape[1]
    codes = phase_ref.shape[0]
    rows = own_ref.shape[0]
    cosine, sine = jnp.cos(phase_ref[...]), jnp.sin(phase_ref[...])
    keys = keys_ref[...]
    leaf_copy.wait()
    real_in, imag_in = leaf_ref[:half_width, :], leaf_ref[half_width:, :]

    def selected(mask):
        picker = jnp.where(mask, 1.0, 0.0).astype(jnp.bfloat16)
        return tuple(
            lax.dot_general(picker, half, (((1,), (1,)), ((), ())), preferred_element_type=jnp.float32)
            for half in (real_in, imag_in)
        )

    code = lax.broadcasted_iota(jnp.int32, (codes, keys.shape[1]), 0)
    real, imag = selected(((keys & (codes - 1)) == code) & (keys < codes * parents_ref[0:1, 0:1]))
    tail_out[0:1, :half_width] = jnp.sum(real * cosine - imag * sine, 0, keepdims=True)
    tail_out[1:2, :half_width] = jnp.sum(real * sine + imag * cosine, 0, keepdims=True)
    tail_copy = copy(tail_out, tail_in, tail_send, tail_recv, left)
    tail_copy.start()

    square = (rows, rows)
    diagonal = lax.broadcasted_iota(jnp.int32, square, 0) == lax.broadcasted_iota(jnp.int32, square, 1)
    parents = jnp.broadcast_to(parents_ref[...].astype(jnp.float32), square)
    column = codes * jnp.sum(jnp.where(diagonal, parents, 0.0), 1, keepdims=True).astype(jnp.int32)
    real, imag = selected(jnp.concatenate([column + c for c in range(codes)], 0) == keys)
    real_sum = jnp.zeros((rows, half_width), jnp.float32)
    imag_sum = jnp.zeros((rows, half_width), jnp.float32)
    for c in range(codes):
        a, b = real[c * rows : (c + 1) * rows], imag[c * rows : (c + 1) * rows]
        real_sum = real_sum + (a * cosine[c : c + 1] - b * sine[c : c + 1])
        imag_sum = imag_sum + (a * sine[c : c + 1] + b * cosine[c : c + 1])
    tail_copy.wait_recv()
    last = lax.broadcasted_iota(jnp.int32, (rows, 1), 0) == rows - 1
    real_sum = real_sum + jnp.where(last, tail_in[0:1, :half_width], 0.0)
    imag_sum = imag_sum + jnp.where(last, tail_in[1:2, :half_width], 0.0)
    gathered = jnp.concatenate([real_sum, imag_sum], 0).astype(jnp.bfloat16)
    coarsen_copy.wait()
    by_real = jnp.dot(gathered, coarsen_ref[0], preferred_element_type=jnp.float32)
    by_imag = jnp.dot(gathered, coarsen_ref[1], preferred_element_type=jnp.float32)
    outs = (by_real[:rows] - by_imag[rows:], by_imag[:rows] + by_real[rows:])
    tiles = own_wide.shape[1] // 2
    padding = jnp.zeros((rows, tiles * LANES - half_width), jnp.float32)
    for part in range(2):
        whole = jnp.concatenate([outs[part], padding], 1)
        for i in range(tiles):
            own_wide[:, part * tiles + i, :] = whole[:, i * LANES : (i + 1) * LANES]
    own_ref[...] = own_wide[...].astype(own_ref.dtype)

    parts = range(PARTS)
    indices = range(len(peers))
    @pl.when(r > 0)
    def _():
        for part in parts:
            along(part).start()
    for part in parts:
        for index in indices:
            @pl.when(peers[index] > r)
            def _():
                far(own_ref, index, part).start()
    @pl.when(lax.rem(r, 2) == 0)
    def _():
        for part in parts:
            near(own_ref, part).start()
    own_copy = pltpu.make_async_copy(own_ref, window_ref.at[r], own_sem)
    own_copy.start()
    for part in range(2):
        up_ref[:, part * half_width : (part + 1) * half_width] = outs[part].astype(up_ref.dtype)

    transfer_copy.wait()
    kinds = transfer_ref.shape[0]
    step = coef_wide.shape[0]

    def lay_out(start, size):
        block = transfer_ref[pl.ds(start, size), :].astype(jnp.float32)
        padding = jnp.zeros((size, tiles * LANES - half_width), jnp.float32)
        for part in range(2):
            whole = jnp.concatenate([block[:, part * half_width : (part + 1) * half_width], padding], 1)
            for i in range(tiles):
                coef_wide[pl.ds(0, size), part * tiles + i, :] = whole[:, i * LANES : (i + 1) * LANES]
        coef[pl.ds(start, size)] = coef_wide[pl.ds(0, size)].astype(coef.dtype)

    def lay_out_step(i, carry):
        lay_out(pl.multiple_of(i * step, step), step)
        return carry

    lax.fori_loop(0, kinds // step, lay_out_step, 0)
    if kinds % step:
        lay_out(kinds // step * step, kinds % step)
    coef[kinds] = jnp.zeros(coef.shape[1:], coef.dtype)
    coef_copy = pltpu.make_async_copy(coef, coef_hbm, coef_sem)
    coef_copy.start()

    sources = vsrc_ref[...]
    slots = sources.shape[1]
    live = sources >= 0
    place = lax.rem(lax.div(sources, rows) + r + 1, group)
    src_ref[...] = jnp.zeros(src_ref.shape, jnp.int32)
    src_ref[:, :slots] = jnp.where(live, place * rows + lax.rem(sources, rows), 0)
    kind_ref[...] = jnp.full(kind_ref.shape, kinds, jnp.int32)
    kind_ref[:, :slots] = jnp.where(live, vtype_ref[...], kinds)
    lengths = jnp.sum(jnp.where(live, 1.0, 0.0), 1, keepdims=True).astype(jnp.int32)
    more_ref[...] = lax.div(jnp.maximum(lengths - fixed + chunk - 1, 0), chunk)
    for part in parts:
        @pl.when(r > 0)
        def _():
            along(part).wait_recv()
        for index in indices:
            @pl.when(peers[index] < r)
            def _():
                far(prev_ref, index, part).start()
        @pl.when(lax.rem(r, 2) == 1)
        def _():
            near(prev_ref, part).start()
    for turn in range(2):
        index = first if turn == 0 else 1 - first
        slot = flip_low + index * (flip_high - flip_low)
        for part in parts:
            arrived(index, slot, part).wait_recv()
            onward(index, slot, part).start()
            @pl.when(late == turn)
            def _():
                across(part).start()
    for part in parts:
        across(part).wait_recv()
        onward(2, flip_both, part).start()
    for part in parts:
        near(own_ref, part).wait_recv()
        for index in range(3):
            onward(index, r, part).wait_recv()
    coef_copy.wait()
    tail_copy.wait_send()
    for part in parts:
        @pl.when(r > 0)
        def _():
            along(part).wait_send()
        near(own_ref, part).wait_send()
        across(part).wait_send()
        for index in indices:
            far(own_ref, index, part).wait_send()
        for index in range(3):
            onward(index, r, part).wait_send()
    own_copy.wait()


def upward_and_window(
    leaf_spectra, leaf_keys, parent_keys, child_phase, coarsen, transfer, vlist_src, vlist_type, axis, group
):
    half_width = child_phase.shape[1]
    rows = parent_keys.shape[0]
    codes = child_phase.shape[0]
    tiles = 2 * (-(-half_width // LANES))
    slots = vlist_src.shape[1]
    fixed = slots // 2 // CHUNK * CHUNK
    padded = -(-slots // CHUNK) * CHUNK
    dma = pltpu.SemaphoreType.DMA
    anywhere = pl.BlockSpec(memory_space=pl.ANY)
    vmem = pl.BlockSpec(memory_space=pltpu.VMEM)
    own = (rows, tiles, LANES)
    coef = (transfer.shape[0] + 1, tiles, LANES)
    upward, window, _, coef, src, kind, more = pl.pallas_call(
        functools.partial(upward_kernel, axis, lax.axis_size(axis), group, fixed, CHUNK),
        out_shape=[
            jax.ShapeDtypeStruct((rows, 2 * half_width), jnp.bfloat16),
            jax.ShapeDtypeStruct((group,) + own, jnp.bfloat16),
            jax.ShapeDtypeStruct(own, jnp.bfloat16),
            jax.ShapeDtypeStruct(coef, jnp.bfloat16),
            jax.ShapeDtypeStruct((rows, padded), jnp.int32),
            jax.ShapeDtypeStruct((rows, padded), jnp.int32),
            jax.ShapeDtypeStruct((rows, 1), jnp.int32),
        ],
        in_specs=[vmem] * 5 + [anywhere] * 3,
        out_specs=[vmem, anywhere, anywhere, anywhere, vmem, vmem, vmem],
        scratch_shapes=[
            pltpu.VMEM(leaf_spectra.shape[::-1], leaf_spectra.dtype),
            pltpu.VMEM(coarsen.shape, coarsen.dtype),
            pltpu.VMEM(transfer.shape, transfer.dtype),
            pltpu.VMEM((2, tiles // 2 * LANES), jnp.float32),
            pltpu.VMEM((2, tiles // 2 * LANES), jnp.float32),
            pltpu.VMEM(own, jnp.float32),
            pltpu.VMEM(own, jnp.bfloat16),
            pltpu.VMEM((16, tiles, LANES), jnp.float32),
            pltpu.VMEM(coef, jnp.bfloat16),
            dma((PARTS,)), dma((PARTS,)),
            dma((2, PARTS)), dma((2, PARTS)),
            dma((PARTS,)), dma((PARTS,)),
            dma((3, PARTS)), dma((3, PARTS)),
            dma((PARTS,)), dma((PARTS,)),
            dma, dma, dma, dma, dma, dma, dma,
        ],
        compiler_params=pltpu.CompilerParams(
            collective_id=0, has_side_effects=True, vmem_limit_bytes=56 * 2**20
        ),
        name="upward_and_window",
    )(
        leaf_keys.reshape(1, -1), parent_keys.reshape(1, -1), child_phase, vlist_src, vlist_type, leaf_spectra.T, coarsen, transfer
    )
    return upward, window, coef, src, kind, more, fixed


def interact_kernel(fixed, chunk, half_width, count_ref, src_ref, kind_ref, table, coef, up_hbm, out_ref, up_out, sums, up_sem):
    up_copy = pltpu.make_async_copy(up_hbm, up_out, up_sem)
    up_copy.start()
    rows = table.shape[1]
    half = rows // 2
    most = (src_ref.shape[1] - fixed) // chunk

    def some_slots(target, count):
        re = [jnp.zeros((half, LANES), jnp.float32)] * CHAINS
        im = [jnp.zeros((half, LANES), jnp.float32)] * CHAINS
        for slot in range(count):
            source = table[src_ref[target, slot]].astype(jnp.float32)
            factor = coef[kind_ref[target, slot]].astype(jnp.float32)
            i = slot % CHAINS
            re[i] = re[i] + (factor[:half] * source[:half] - factor[half:] * source[half:])
            im[i] = im[i] + (factor[:half] * source[half:] + factor[half:] * source[:half])
        sums[target, :half] = sum(re[1:], re[0])
        sums[target, half:] = sum(im[1:], im[0])

    def one_target(target, carry):
        def between(low, high):
            if low == high:
                some_slots(target, fixed + low * chunk)
                return
            middle = (low + high) // 2
            lax.cond(more <= middle, lambda: between(low, middle), lambda: between(middle + 1, high))

        more = count_ref[target, 0]
        between(0, most)
        return carry

    lax.fori_loop(0, src_ref.shape[0], one_target, 0)
    for part in range(2):
        pieces = [sums[:, part * half + i, :] for i in range(half)]
        whole = jnp.concatenate(pieces, 1)[:, :half_width]
        out_ref[:, part * half_width : (part + 1) * half_width] = whole.astype(out_ref.dtype)
    up_copy.wait()


def interact(window, coef, src, kind, more, fixed, upward):
    targets = src.shape[0]
    smem = pl.BlockSpec(memory_space=pltpu.SMEM)
    vmem = pl.BlockSpec(memory_space=pltpu.VMEM)
    anywhere = pl.BlockSpec(memory_space=pl.ANY)
    return pl.pallas_call(
        functools.partial(interact_kernel, fixed, CHUNK, upward.shape[1] // 2),
        out_shape=[jax.ShapeDtypeStruct(upward.shape, jnp.bfloat16)] * 2,
        in_specs=[smem, smem, smem, vmem, vmem, anywhere],
        out_specs=[vmem, anywhere],
        scratch_shapes=[
            pltpu.VMEM((targets, window.shape[1], LANES), jnp.float32),
            pltpu.SemaphoreType.DMA,
        ],
        compiler_params=pltpu.CompilerParams(vmem_limit_bytes=56 * 2**20),
        name="interact",
    )(more, src, kind, window, coef, upward)


def shards(
    leaf_spectra, leaf_keys, parent_keys, child_phase, coarsen, transfer, vlist_src, vlist_type
):
    group = 2**GBITS
    upward, window, coef, src, kind, more, fixed = upward_and_window(
        leaf_spectra, leaf_keys, parent_keys, child_phase, coarsen, transfer, vlist_src, vlist_type, "oct", group
    )
    rows = parent_keys.shape[0]
    window = window.reshape((group * rows,) + window.shape[2:])
    local_field, upward = interact(window, coef, src, kind, more, fixed, upward)
    return (upward, local_field)


def solution(mesh):
    return jax.shard_map(
        shards,
        mesh=mesh,
        in_specs=(
            P("oct", None),
            P("oct"),
            P("oct"),
            P(),
            P(),
            P(),
            P("oct", None),
            P("oct", None),
        ),
        out_specs=(P("oct", None), P("oct", None)),
        check_vma=False,
    )
```

```python
import functools
import jax
import jax.numpy as jnp
from jax import lax
from jax.experimental import pallas as pl
from jax.experimental.pallas import tpu as pltpu
from jax.sharding import PartitionSpec as P

GBITS = 3
LANES = 128
CHUNK = 16
PARTS = 4


def upward_kernel(
    axis, count, group, fixed, chunk, keys_ref, parents_ref, phase_ref, vsrc_ref, vtype_ref, leaf_hbm, coarsen_hbm,
    transfer_hbm, up_ref, window_ref, prev_ref, coef_hbm, src_ref, kind_ref, more_ref,
    leaf_ref, coarsen_ref, transfer_ref, tail_out, tail_in, own_wide, own_ref, coef_wide, coef, *sems
):
    (z_send, z_recv, far_send, far_recv, near_send, near_recv, pass_send, pass_recv,
     across_send, across_recv, own_sem, leaf_sem, coarsen_sem, transfer_sem, coef_sem, tail_send, tail_recv) = sems
    leaf_copy = pltpu.make_async_copy(leaf_hbm, leaf_ref, leaf_sem)
    leaf_copy.start()
    coarsen_copy = pltpu.make_async_copy(coarsen_hbm, coarsen_ref, coarsen_sem)
    coarsen_copy.start()
    transfer_copy = pltpu.make_async_copy(transfer_hbm, transfer_ref, transfer_sem)
    transfer_copy.start()
    me = lax.axis_index(axis)
    r = lax.rem(me, group)
    base = me - r
    after = lax.rem(me + group, count)
    before = lax.rem(me + count - group, count)
    twin = me + 1 - 2 * lax.rem(r, 2)
    core = lax.rem(r, 2)
    chip = lax.div(r, 2)
    flip_low = r + 2 - 4 * lax.rem(chip, 2)
    flip_high = r + 4 - 8 * lax.div(chip, 2)
    flip_both = flip_low + flip_high - r
    peers = (flip_low, flip_high)
    is_one = jnp.where(chip == 1, 1, 0)
    is_two = jnp.where(chip == 2, 1, 0)
    first = 1 - is_one
    passed = 2 * (2 - 2 * is_one - 2 * is_two - lax.div(chip, 3) + 3 * (is_one * core + is_two * (1 - core))) + core
    late = is_one * core + is_two * (1 - core)
    piece = own_ref.shape[0] // PARTS

    barrier = pltpu.get_barrier_semaphore()
    left, right = lax.rem(me + count - 1, count), lax.rem(me + 1, count)
    greeted = [after, before, twin, left, right] + [base + peer for peer in peers]
    for device in greeted:
        pl.semaphore_signal(barrier, inc=1, device_id={axis: device}, device_id_type=pl.DeviceIdType.MESH)
    pl.semaphore_wait(barrier, len(greeted))

    def copy(source, target, send, recv, device):
        return pltpu.make_async_remote_copy(
            src_ref=source, dst_ref=target, send_sem=send, recv_sem=recv,
            device_id={axis: device}, device_id_type=pl.DeviceIdType.MESH,
        )

    def rows_of(part):
        return pl.ds(part * piece, piece)

    def along(part):
        return copy(own_ref.at[rows_of(part)], prev_ref.at[rows_of(part)], z_send.at[part], z_recv.at[part], after)

    def far(block, index, part):
        return copy(
            block.at[rows_of(part)], window_ref.at[r, rows_of(part)],
            far_send.at[index, part], far_recv.at[index, part], base + peers[index],
        )

    def near(block, part):
        return copy(
            block.at[rows_of(part)], window_ref.at[r, rows_of(part)], near_send.at[part], near_recv.at[part], twin
        )

    def arrived(index, slot, part):
        here = window_ref.at[slot, rows_of(part)]
        return copy(here, here, far_send.at[0, part], far_recv.at[index, part], twin)

    def across(part):
        here = window_ref.at[passed, rows_of(part)]
        there = base + 2 * (3 - lax.div(passed, 2)) + core
        return copy(here, here, across_send.at[part], across_recv.at[part], there)

    def onward(index, slot, part):
        here = window_ref.at[slot, rows_of(part)]
        return copy(here, here, pass_send.at[index, part], pass_recv.at[index, part], twin)

    half_width = phase_ref.shape[1]
    codes = phase_ref.shape[0]
    rows = own_ref.shape[0]
    cosine, sine = jnp.cos(phase_ref[...]), jnp.sin(phase_ref[...])
    keys = keys_ref[...]
    leaf_copy.wait()
    real_in, imag_in = leaf_ref[:half_width, :], leaf_ref[half_width:, :]

    def selected(mask):
        picker = jnp.where(mask, 1.0, 0.0).astype(jnp.bfloat16)
        return tuple(
            lax.dot_general(picker, half, (((1,), (1,)), ((), ())), preferred_element_type=jnp.float32)
            for half in (real_in, imag_in)
        )

    code = lax.broadcasted_iota(jnp.int32, (codes, keys.shape[1]), 0)
    real, imag = selected(((keys & (codes - 1)) == code) & (keys < codes * parents_ref[0:1, 0:1]))
    tail_out[0:1, :half_width] = jnp.sum(real * cosine - imag * sine, 0, keepdims=True)
    tail_out[1:2, :half_width] = jnp.sum(real * sine + imag * cosine, 0, keepdims=True)
    tail_copy = copy(tail_out, tail_in, tail_send, tail_recv, left)
    tail_copy.start()

    square = (rows, rows)
    diagonal = lax.broadcasted_iota(jnp.int32, square, 0) == lax.broadcasted_iota(jnp.int32, square, 1)
    parents = jnp.broadcast_to(parents_ref[...].astype(jnp.float32), square)
    column = codes * jnp.sum(jnp.where(diagonal, parents, 0.0), 1, keepdims=True).astype(jnp.int32)
    real, imag = selected(jnp.concatenate([column + c for c in range(codes)], 0) == keys)
    real_sum = jnp.zeros((rows, half_width), jnp.float32)
    imag_sum = jnp.zeros((rows, half_width), jnp.float32)
    for c in range(codes):
        a, b = real[c * rows : (c + 1) * rows], imag[c * rows : (c + 1) * rows]
        real_sum = real_sum + (a * cosine[c : c + 1] - b * sine[c : c + 1])
        imag_sum = imag_sum + (a * sine[c : c + 1] + b * cosine[c : c + 1])
    tail_copy.wait_recv()
    last = lax.broadcasted_iota(jnp.int32, (rows, 1), 0) == rows - 1
    real_sum = real_sum + jnp.where(last, tail_in[0:1, :half_width], 0.0)
    imag_sum = imag_sum + jnp.where(last, tail_in[1:2, :half_width], 0.0)
    gathered = jnp.concatenate([real_sum, imag_sum], 0).astype(jnp.bfloat16)
    coarsen_copy.wait()
    by_real = jnp.dot(gathered, coarsen_ref[0], preferred_element_type=jnp.float32)
    by_imag = jnp.dot(gathered, coarsen_ref[1], preferred_element_type=jnp.float32)
    outs = (by_real[:rows] - by_imag[rows:], by_imag[:rows] + by_real[rows:])
    tiles = own_wide.shape[1] // 2
    padding = jnp.zeros((rows, tiles * LANES - half_width), jnp.float32)
    for part in range(2):
        whole = jnp.concatenate([outs[part], padding], 1)
        for i in range(tiles):
            own_wide[:, part * tiles + i, :] = whole[:, i * LANES : (i + 1) * LANES]
    own_ref[...] = own_wide[...].astype(own_ref.dtype)

    parts = range(PARTS)
    indices = range(len(peers))
    @pl.when(r > 0)
    def _():
        for part in parts:
            along(part).start()
    for part in parts:
        for index in indices:
            @pl.when(peers[index] > r)
            def _():
                far(own_ref, index, part).start()
    @pl.when(lax.rem(r, 2) == 0)
    def _():
        for part in parts:
            near(own_ref, part).start()
    own_copy = pltpu.make_async_copy(own_ref, window_ref.at[r], own_sem)
    own_copy.start()
    for part in range(2):
        up_ref[:, part * half_width : (part + 1) * half_width] = outs[part].astype(up_ref.dtype)

    transfer_copy.wait()
    kinds = transfer_ref.shape[0]
    step = coef_wide.shape[0]

    def lay_out(start, size):
        block = transfer_ref[pl.ds(start, size), :].astype(jnp.float32)
        padding = jnp.zeros((size, tiles * LANES - half_width), jnp.float32)
        for part in range(2):
            whole = jnp.concatenate([block[:, part * half_width : (part + 1) * half_width], padding], 1)
            for i in range(tiles):
                coef_wide[pl.ds(0, size), part * tiles + i, :] = whole[:, i * LANES : (i + 1) * LANES]
        coef[pl.ds(start, size)] = coef_wide[pl.ds(0, size)].astype(coef.dtype)

    def lay_out_step(i, carry):
        lay_out(pl.multiple_of(i * step, step), step)
        return carry

    lax.fori_loop(0, kinds // step, lay_out_step, 0)
    if kinds % step:
        lay_out(kinds // step * step, kinds % step)
    coef[kinds] = jnp.zeros(coef.shape[1:], coef.dtype)
    coef_copy = pltpu.make_async_copy(coef, coef_hbm, coef_sem)
    coef_copy.start()

    sources = vsrc_ref[...]
    slots = sources.shape[1]
    live = sources >= 0
    place = lax.rem(lax.div(sources, rows) + r + 1, group)
    src_ref[...] = jnp.zeros(src_ref.shape, jnp.int32)
    src_ref[:, :slots] = jnp.where(live, place * rows + lax.rem(sources, rows), 0)
    kind_ref[...] = jnp.full(kind_ref.shape, kinds, jnp.int32)
    kind_ref[:, :slots] = jnp.where(live, vtype_ref[...], kinds)
    lengths = jnp.sum(jnp.where(live, 1.0, 0.0), 1, keepdims=True).astype(jnp.int32)
    more_ref[...] = lax.div(jnp.maximum(lengths - fixed + chunk - 1, 0), chunk)
    for part in parts:
        @pl.when(r > 0)
        def _():
            along(part).wait_recv()
        for index in indices:
            @pl.when(peers[index] < r)
            def _():
                far(prev_ref, index, part).start()
        @pl.when(lax.rem(r, 2) == 1)
        def _():
            near(prev_ref, part).start()
    for turn in range(2):
        index = first if turn == 0 else 1 - first
        slot = flip_low + index * (flip_high - flip_low)
        for part in parts:
            arrived(index, slot, part).wait_recv()
            onward(index, slot, part).start()
            @pl.when(late == turn)
            def _():
                across(part).start()
    for part in parts:
        across(part).wait_recv()
        onward(2, flip_both, part).start()
    for part in parts:
        near(own_ref, part).wait_recv()
        for index in range(3):
            onward(index, r, part).wait_recv()
    coef_copy.wait()
    tail_copy.wait_send()
    for part in parts:
        @pl.when(r > 0)
        def _():
            along(part).wait_send()
        near(own_ref, part).wait_send()
        across(part).wait_send()
        for index in indices:
            far(own_ref, index, part).wait_send()
        for index in range(3):
            onward(index, r, part).wait_send()
    own_copy.wait()


def upward_and_window(
    leaf_spectra, leaf_keys, parent_keys, child_phase, coarsen, transfer, vlist_src, vlist_type, axis, group
):
    half_width = child_phase.shape[1]
    rows = parent_keys.shape[0]
    codes = child_phase.shape[0]
    tiles = 2 * (-(-half_width // LANES))
    slots = vlist_src.shape[1]
    fixed = slots // 2 // CHUNK * CHUNK
    padded = -(-slots // CHUNK) * CHUNK
    dma = pltpu.SemaphoreType.DMA
    anywhere = pl.BlockSpec(memory_space=pl.ANY)
    vmem = pl.BlockSpec(memory_space=pltpu.VMEM)
    own = (rows, tiles, LANES)
    coef = (transfer.shape[0] + 1, tiles, LANES)
    upward, window, _, coef, src, kind, more = pl.pallas_call(
        functools.partial(upward_kernel, axis, lax.axis_size(axis), group, fixed, CHUNK),
        out_shape=[
            jax.ShapeDtypeStruct((rows, 2 * half_width), jnp.bfloat16),
            jax.ShapeDtypeStruct((group,) + own, jnp.bfloat16),
            jax.ShapeDtypeStruct(own, jnp.bfloat16),
            jax.ShapeDtypeStruct(coef, jnp.bfloat16),
            jax.ShapeDtypeStruct((rows, padded), jnp.int32),
            jax.ShapeDtypeStruct((rows, padded), jnp.int32),
            jax.ShapeDtypeStruct((rows, 1), jnp.int32),
        ],
        in_specs=[vmem] * 5 + [anywhere] * 3,
        out_specs=[vmem, anywhere, anywhere, anywhere, vmem, vmem, vmem],
        scratch_shapes=[
            pltpu.VMEM(leaf_spectra.shape[::-1], leaf_spectra.dtype),
            pltpu.VMEM(coarsen.shape, coarsen.dtype),
            pltpu.VMEM(transfer.shape, transfer.dtype),
            pltpu.VMEM((2, tiles // 2 * LANES), jnp.float32),
            pltpu.VMEM((2, tiles // 2 * LANES), jnp.float32),
            pltpu.VMEM(own, jnp.float32),
            pltpu.VMEM(own, jnp.bfloat16),
            pltpu.VMEM((16, tiles, LANES), jnp.float32),
            pltpu.VMEM(coef, jnp.bfloat16),
            dma((PARTS,)), dma((PARTS,)),
            dma((2, PARTS)), dma((2, PARTS)),
            dma((PARTS,)), dma((PARTS,)),
            dma((3, PARTS)), dma((3, PARTS)),
            dma((PARTS,)), dma((PARTS,)),
            dma, dma, dma, dma, dma, dma, dma,
        ],
        compiler_params=pltpu.CompilerParams(
            collective_id=0, has_side_effects=True, vmem_limit_bytes=56 * 2**20
        ),
        name="upward_and_window",
    )(
        leaf_keys.reshape(1, -1), parent_keys.reshape(1, -1), child_phase, vlist_src, vlist_type, leaf_spectra.T, coarsen, transfer
    )
    return upward, window, coef, src, kind, more, fixed


def interact_kernel(fixed, chunk, half_width, count_ref, src_ref, kind_ref, table, coef, up_ref, out_ref, up_out, sums):
    up_out[...] = up_ref[...]
    rows = table.shape[1]
    half = rows // 2
    most = (src_ref.shape[1] - fixed) // chunk

    def some_slots(target, count):
        re = jnp.zeros((half, LANES), jnp.float32)
        im = jnp.zeros((half, LANES), jnp.float32)
        for slot in range(count):
            source = table[src_ref[target, slot]].astype(jnp.float32)
            factor = coef[kind_ref[target, slot]].astype(jnp.float32)
            re = re + (factor[:half] * source[:half] - factor[half:] * source[half:])
            im = im + (factor[:half] * source[half:] + factor[half:] * source[:half])
        sums[target, :half] = re
        sums[target, half:] = im

    def one_target(target, carry):
        def between(low, high):
            if low == high:
                some_slots(target, fixed + low * chunk)
                return
            middle = (low + high) // 2
            lax.cond(more <= middle, lambda: between(low, middle), lambda: between(middle + 1, high))

        more = count_ref[target, 0]
        between(0, most)
        return carry

    lax.fori_loop(0, src_ref.shape[0], one_target, 0)
    for part in range(2):
        pieces = [sums[:, part * half + i, :] for i in range(half)]
        whole = jnp.concatenate(pieces, 1)[:, :half_width]
        out_ref[:, part * half_width : (part + 1) * half_width] = whole.astype(out_ref.dtype)


def interact(window, coef, src, kind, more, fixed, upward):
    targets = src.shape[0]
    smem = pl.BlockSpec(memory_space=pltpu.SMEM)
    vmem = pl.BlockSpec(memory_space=pltpu.VMEM)
    return pl.pallas_call(
        functools.partial(interact_kernel, fixed, CHUNK, upward.shape[1] // 2),
        out_shape=[jax.ShapeDtypeStruct(upward.shape, jnp.bfloat16)] * 2,
        in_specs=[smem, smem, smem, vmem, vmem, vmem],
        out_specs=[vmem, vmem],
        scratch_shapes=[pltpu.VMEM((targets, window.shape[1], LANES), jnp.float32)],
        compiler_params=pltpu.CompilerParams(vmem_limit_bytes=56 * 2**20),
        name="interact",
    )(more, src, kind, window, coef, upward)


def shards(
    leaf_spectra, leaf_keys, parent_keys, child_phase, coarsen, transfer, vlist_src, vlist_type
):
    group = 2**GBITS
    upward, window, coef, src, kind, more, fixed = upward_and_window(
        leaf_spectra, leaf_keys, parent_keys, child_phase, coarsen, transfer, vlist_src, vlist_type, "oct", group
    )
    rows = parent_keys.shape[0]
    window = window.reshape((group * rows,) + window.shape[2:])
    local_field, upward = interact(window, coef, src, kind, more, fixed, upward)
    return (upward, local_field)


def solution(mesh):
    return jax.shard_map(
        shards,
        mesh=mesh,
        in_specs=(
            P("oct", None),
            P("oct"),
            P("oct"),
            P(),
            P(),
            P(),
            P("oct", None),
            P("oct", None),
        ),
        out_specs=(P("oct", None), P("oct", None)),
        check_vma=False,
    )
```
